32 devices in a mesh: grp: 16 (over z, y, x), fold: 2 (over core).
Axes of the slice: x: 2, y: 2, z: 4, core: 2. Of those that a mesh axis runs over, the one named last changes fastest.
Arguments:
- blocks: bfloat16 [9, 2, 64, 64, 2048], P(None, None, 'fold', None, 'grp'), may hold values from -30 to 30
- source: bfloat16 [2, 64, 12, 2048], P(None, 'fold', None, 'grp'), may hold values from -8 to 8
- plane_counts: int32 [16], P('grp'), may hold values from 1 to 2, 24 in all
Outputs:
- solution: float32 [2, 64, 12, 2048], P(None, 'fold', None, 'grp')
- residual: float32 [2, 64, 12, 2048], P(None, 'fold', None, 'grp')
The draws below stay inside these ranges and needn't reach their ends.
Inputs may be any that keep to these rules, and one draw needn't show every extreme that they name: plane_counts sum to 24; the busiest group holds exactly 2 planes.
All inputs are finite; a program needn't handle non-finite values.
Results may differ from the reference program's by a relative error of at most 0.0032.
Values may be sent and summed in bfloat16 or wider, within the bound.
A program may use at most 128 MiB of HBM per device.

```python
import math
import jax
import jax.numpy as jnp
import numpy as np

NCOMP = 64
NRHS = 12
LX = 4
LY = 4
LT = 4
SWEEPS = 2
CAP = 2
PLANE = 64
SITES = 2048
NZ = 24
N_GRP = 16


def draw_blocks(key, part):
    first_key = jax.random.fold_in(key, 11)
    second_key = jax.random.fold_in(key, 12)
    third_key = jax.random.fold_in(key, 13)
    fourth_key = jax.random.fold_in(key, 14)
    fifth_key = jax.random.fold_in(key, 15)
    shape_full = (9, 2, NCOMP, NCOMP, SITES)
    jitter = jax.random.truncated_normal(first_key, -4.0, 4.0, shape_full, jnp.float32)
    hop_scale = jnp.where(jnp.arange(9) == 0, 0.04, 0.015).astype(jnp.float32).reshape(9, 1, 1, 1, 1)
    diagonal = jax.random.uniform(second_key, (NCOMP, SITES), jnp.float32, 1.5, 3.0)
    diagonal_imag = jax.random.uniform(third_key, (NCOMP, SITES), jnp.float32, 0.0, 1.2)
    identity = jnp.eye(NCOMP, dtype=jnp.float32)
    result = jitter * hop_scale
    result = result.at[0, 0].add(identity[:, :, None] * diagonal[:, None, :])
    result = result.at[0, 1].add(identity[:, :, None] * diagonal_imag[:, None, :])
    groups = SITES // (CAP * PLANE)
    ramp = 1.0 + 2.0 * jnp.arange(groups).astype(jnp.float32) / max(groups - 1, 1)
    group_factor = jnp.exp(jax.random.uniform(fourth_key, (groups,), jnp.float32, math.log(0.6), math.log(1.6)))
    group_of = (jnp.arange(SITES) // (CAP * PLANE)).astype(jnp.int32)
    site_scale = (ramp * group_factor)[group_of]
    row_factor = jnp.exp(jax.random.uniform(fifth_key, (NCOMP,), jnp.float32, math.log(0.6), math.log(1.6)))
    return (result * site_scale.reshape(1, 1, 1, 1, SITES) * row_factor.reshape(1, 1, NCOMP, 1, 1)).astype(jnp.bfloat16)


def draw_source(key, part):
    first_key = jax.random.fold_in(key, 21)
    shape_full = (2, NCOMP, NRHS, SITES)
    return jax.random.truncated_normal(first_key, -5.0, 5.0, shape_full, jnp.float32).astype(jnp.bfloat16)


def split_up(count, total, most, lean):
    loads = [(1 << 20) // math.isqrt(rank ** lean) + 1 for rank in range(2, count + 1)]
    spare, counts = total - most - (count - 1), [1] * (count - 1)
    while spare > 0:
        movable = [i for i in range(count - 1) if counts[i] < most]
        whole, left = sum([loads[i] for i in movable]), spare
        for i in movable:
            extra = min(most - counts[i], max(1, left * loads[i] // whole), spare)
            counts[i] = counts[i] + extra
            spare = spare - extra
    return np.array([most] + counts)


def ragged(stream_key, amount, total, most, slope):
    if amount == 2:
        one = jax.random.randint(stream_key, (), max(1, total - most), min(most, total - 1) + 1)
        return jnp.stack([one, total - one])
    sizes = jnp.asarray(split_up(amount, total, most, slope), jnp.int32)
    twos = (amount - 1) // 2
    donor, taker = sizes[1:1 + 2 * twos:2], sizes[2:2 + 2 * twos:2]
    room = jnp.minimum(donor - 1, most - taker)
    passed = jax.random.randint(jax.random.fold_in(stream_key, 1), (twos,), 0, 1 << 20) % (room + 1)
    sizes = sizes.at[1:1 + 2 * twos:2].set(donor - passed).at[2:2 + 2 * twos:2].set(taker + passed)
    return sizes[jax.random.permutation(jax.random.fold_in(stream_key, 2), amount)]


def setup_inputs(seed: int = 0) -> dict:
    key_list = jax.random.split(jax.random.key(seed), 4)
    return {
        "blocks": draw_blocks(jax.random.fold_in(key_list[3], 71), 0),
        "source": draw_source(jax.random.fold_in(key_list[3], 71), 0),
        "plane_counts": ragged(key_list[2], N_GRP, NZ, CAP, 2).astype(jnp.int32),
    }


def complex_apply(block_pair, vector):
    first = block_pair[0].astype(jnp.float32)
    second = block_pair[1].astype(jnp.float32)
    vec_real = vector[0].astype(jnp.float32)
    vec_imag = vector[1].astype(jnp.float32)
    real_part = jnp.einsum("rcs,cks->rks", first, vec_real) - jnp.einsum("rcs,cks->rks", second, vec_imag)
    imag_part = jnp.einsum("rcs,cks->rks", first, vec_imag) + jnp.einsum("rcs,cks->rks", second, vec_real)
    return jnp.stack([real_part, imag_part])


def reference(blocks, source, plane_counts):
    group_count = plane_counts.shape[0]
    plane_sites = LX * LY * LT
    slot_index = jnp.arange(group_count * CAP).astype(jnp.int32)
    group_of = slot_index // CAP
    plane_slot = slot_index % CAP
    prior = (group_of - 1) % group_count
    later = (group_of + 1) % group_count
    lower_index = jnp.where(plane_slot > 0, slot_index - 1, prior * CAP + plane_counts[prior] - 1).astype(jnp.int32)
    upper_index = jnp.where(plane_slot < plane_counts[group_of] - 1, slot_index + 1, later * CAP).astype(jnp.int32)
    live_mask = jnp.repeat((plane_slot < plane_counts[group_of]).astype(jnp.float32), plane_sites)

    def operate(rounded):
        leading = rounded.shape[:3]
        flat_shape = leading + (group_count * CAP * plane_sites,)
        by_plane = rounded.reshape(leading + (group_count * CAP, plane_sites))
        lattice = rounded.reshape(leading + (group_count * CAP, LX, LY, LT))
        neighbours = [rounded]
        for axis_index in (4, 5):
            neighbours.append(jnp.roll(lattice, -1, axis_index).reshape(flat_shape))
            neighbours.append(jnp.roll(lattice, 1, axis_index).reshape(flat_shape))
        neighbours.append(jnp.take(by_plane, upper_index, axis=3).reshape(flat_shape))
        neighbours.append(jnp.take(by_plane, lower_index, axis=3).reshape(flat_shape))
        neighbours.append(jnp.roll(lattice, -1, 6).reshape(flat_shape))
        neighbours.append(jnp.roll(lattice, 1, 6).reshape(flat_shape))
        summed = complex_apply(blocks[0], neighbours[0])
        for hop_index in range(1, 9):
            summed = summed + complex_apply(blocks[hop_index], neighbours[hop_index])
        return summed * live_mask

    residual = source.astype(jnp.float32) * live_mask
    solution = jnp.zeros_like(residual)
    for sweep_index in range(SWEEPS):
        rounded = residual.astype(jnp.bfloat16)
        applied = operate(rounded)
        intersection_re = jnp.sum(applied[0] * residual[0] + applied[1] * residual[1], axis=(0, 2))
        intersection_im = jnp.sum(applied[0] * residual[1] - applied[1] * residual[0], axis=(0, 2))
        image_norm = jnp.sum(applied * applied, axis=(0, 1, 3))
        alpha_re = (intersection_re / image_norm)[:, None]
        alpha_im = (intersection_im / image_norm)[:, None]
        solution = solution + jnp.stack([alpha_re * residual[0] - alpha_im * residual[1], alpha_re * residual[1] + alpha_im * residual[0]])
        residual = residual - jnp.stack([alpha_re * applied[0] - alpha_im * applied[1], alpha_re * applied[1] + alpha_im * applied[0]])
    return solution, residual
```

```python
import functools

import jax
import jax.numpy as jnp
import numpy as np
from jax import lax
from jax.experimental import pallas as pl
from jax.experimental.pallas import tpu as pltpu
from jax.sharding import PartitionSpec as P

SWEEPS = 2
CHUNK = 8
GROUPS = 16
HALF = GROUPS // 2
LOCAL = (0, 1, 2, 3, 4, 7, 8)
ACROSS = (5, 6)
MESH = pl.DeviceIdType.MESH


def lane_moves():
    moves = np.zeros((256, 512), np.float32)
    for lane in range(128):
        base, site = lane // 8 * 8, lane % 8
        low = site < 4
        moves[base + (site ^ 4) + (0 if low else 128), lane] = 1
        moves[base + (site ^ 4) + (128 if low else 0), 128 + lane] = 1
        moves[base + (site & 4) + ((site + 1) & 3), 256 + lane] = 1
        moves[base + (site & 4) + ((site - 1) & 3), 384 + lane] = 1
    return jnp.asarray(moves, jnp.bfloat16)


def kernel(n_grp, n_fold, counts, blocks, source, moves, sol_out, res_out,
           raw, w_local, w_across, res, sol, image, gath, last, rims, local_rhs, red,
           load_sem, x_send, x_recv, r_send, r_recv, s_send, s_recv):
    bf16, f32 = jnp.bfloat16, jnp.float32
    rows, comps = blocks.shape[2], blocks.shape[3]
    nrhs = source.shape[1]
    total = n_grp * n_fold
    grp, fold = lax.axis_index("grp"), lax.axis_index("fold")
    me = grp * n_fold + fold
    loads = [pltpu.make_async_copy(blocks.at[m], raw.at[m], load_sem.at[m]) for m in range(9)]
    for load in loads:
        load.start()

    def device(index):
        return (lax.div(index, n_fold), lax.rem(index, n_fold))

    barrier = pltpu.get_barrier_semaphore()

    def greet(d, carry):
        pl.semaphore_signal(barrier, inc=1, device_id=device(lax.rem(me + d, total)), device_id_type=MESH)
        return carry

    lax.fori_loop(1, total, greet, 0)

    live = (counts[0] - 1).astype(f32)
    lane = lax.broadcasted_iota(jnp.int32, (rows, 128), 1)

    for p in range(2):
        planes = [source[p, k].astype(f32) for k in range(nrhs)]
        for g in range(GROUPS):
            value = jnp.zeros((rows, 128), f32)
            for k in range(nrhs):
                shift = 8 * (k - g) % 128
                moved = planes[k] if shift == 0 else pltpu.roll(planes[k], shift, 1)
                value = jnp.where(lane // 8 == k, moved, value)
            if g >= HALF:
                value = value * live
            res[g, :, 128 * p:128 * p + 128] = value

    pl.semaphore_wait(barrier, total - 1)

    def send_parts(sweep):
        def fill(h, carry):
            lower, upper = res[h], res[h + HALF]
            gath[sweep, fold, h] = lower.astype(bf16)
            gath[sweep, fold, h + HALF] = upper.astype(bf16)
            last[sweep, h] = (upper * live + lower * (1.0 - live)).astype(bf16)
            return carry

        lax.fori_loop(0, HALF, fill, 0)
        gathers, edges = [], []
        for d in range(1, n_fold):
            gathers.append(pltpu.make_async_remote_copy(
                src_ref=gath.at[sweep, fold], dst_ref=gath.at[sweep, fold],
                send_sem=x_send.at[sweep, d], recv_sem=x_recv.at[sweep, d],
                device_id=(grp, lax.rem(fold + d, n_fold)), device_id_type=MESH))
        for d in range(n_fold):
            other = lax.rem(fold + d, n_fold)
            edges.append(pltpu.make_async_remote_copy(
                src_ref=gath.at[sweep, fold, pl.ds(0, HALF)], dst_ref=rims.at[sweep, 0, fold],
                send_sem=r_send.at[sweep, 0, d], recv_sem=r_recv.at[sweep, 0, d],
                device_id=(lax.rem(grp + n_grp - 1, n_grp), other), device_id_type=MESH))
            edges.append(pltpu.make_async_remote_copy(
                src_ref=last.at[sweep], dst_ref=rims.at[sweep, 1, fold],
                send_sem=r_send.at[sweep, 1, d], recv_sem=r_recv.at[sweep, 1, d],
                device_id=(lax.rem(grp + 1, n_grp), other), device_id_type=MESH))
        for copy in gathers + edges:
            copy.start()
        return gathers, edges

    def wait_gather(sweep):
        for d in range(1, n_fold):
            sender = lax.rem(fold + n_fold - d, n_fold)
            slot = gath.at[sweep, sender]
            pltpu.make_async_remote_copy(
                src_ref=slot, dst_ref=slot, send_sem=x_send.at[sweep, d], recv_sem=x_recv.at[sweep, d],
                device_id=(grp, lax.rem(fold + d, n_fold)), device_id_type=MESH).wait_recv()

    def wait_edges(sweep):
        for side in range(2):
            for d in range(n_fold):
                sender = lax.rem(fold + n_fold - d, n_fold)
                slot = rims.at[sweep, side, sender]
                pltpu.make_async_remote_copy(
                    src_ref=slot, dst_ref=slot, send_sem=r_send.at[sweep, side, d],
                    recv_sem=r_recv.at[sweep, side, d],
                    device_id=(lax.rem(grp + 1, n_grp), fold), device_id_type=MESH).wait_recv()

    def whole_rows(read):
        parts = [read(f) for f in range(n_fold)]
        if rows % 16:
            return jnp.concatenate([part.astype(f32) for part in parts], axis=0).astype(bf16)
        return jnp.concatenate(parts, axis=0)

    def doubled(re, im):
        return jnp.concatenate(
            [jnp.concatenate([re, im], axis=1), jnp.concatenate([-im, re], axis=1)], axis=0)

    def build_local(sweep):
        def pair(h, carry):
            chunks = [whole_rows(lambda f, i=i: gath[sweep, f, 2 * h + i]) for i in range(2)]
            (are, aim), (bre, bim) = [(c[:, :128], c[:, 128:]) for c in chunks]
            local_rhs[0, 2 * h] = doubled(are, aim)
            local_rhs[0, 2 * h + 1] = doubled(bre, bim)
            left = jnp.concatenate([jnp.concatenate([are, aim, bre, bim], axis=0),
                                    jnp.concatenate([bre, bim, are, aim], axis=0)], axis=1)
            moved = jnp.dot(left, moves[...], preferred_element_type=f32).astype(bf16)
            for i in range(2):
                for hop in range(4):
                    cut = moved[2 * comps * i:2 * comps * (i + 1), 128 * hop:128 * hop + 128]
                    local_rhs[1 + hop, 2 * h + i] = doubled(cut[:comps], cut[comps:])
            return carry

        lax.fori_loop(0, HALF, pair, 0)

    row_site = lax.broadcasted_iota(jnp.int32, (rows * CHUNK, 256), 0) % CHUNK
    lane_site = lax.broadcasted_iota(jnp.int32, (rows * CHUNK, 256), 1) % CHUNK

    def same_site(product):
        kept = jnp.where(row_site == lane_site, product, 0.0)
        return jnp.sum(kept.reshape(rows, CHUNK, 256), axis=1)

    def apply_local():
        def chunk(g, carry):
            plane, x, low = g // HALF * HALF, g % HALF // 2, g % 2
            ahead, behind = plane + (x + 1) % 4 * 2 + low, plane + (x + 3) % 4 * 2 + low
            rhs = jnp.concatenate(
                [local_rhs[0, g], local_rhs[0, ahead], local_rhs[0, behind]]
                + [local_rhs[1 + hop, g] for hop in range(4)], axis=0)
            image[g] = same_site(jnp.dot(w_local[g], rhs, preferred_element_type=f32))
            return carry

        lax.fori_loop(0, GROUPS, chunk, 0)

    def dots(a, r):
        are, aim, rre, rim = a[:, :128], a[:, 128:], r[:, :128], r[:, 128:]
        return are * rre + aim * rim, are * rim - aim * rre, are * are + aim * aim

    def apply_across(sweep):
        def plane_chunk(h, sums):
            after = whole_rows(lambda f: rims[sweep, 0, f, h])
            before = whole_rows(lambda f: rims[sweep, 1, f, h])
            after = doubled(after[:, :128], after[:, 128:])
            before = doubled(before[:, :128], before[:, 128:])
            inner, outer = local_rhs[0, h], local_rhs[0, h + HALF]
            up = (outer.astype(f32) * live + after.astype(f32) * (1.0 - live)).astype(bf16)
            first = same_site(jnp.dot(w_across[h], jnp.concatenate([up, before], axis=0),
                                      preferred_element_type=f32))
            second = same_site(jnp.dot(w_across[h + HALF], jnp.concatenate([after, inner], axis=0),
                                       preferred_element_type=f32))
            first = first + image[h]
            second = (second + image[h + HALF]) * live
            image[h] = first
            image[h + HALF] = second
            one, two = dots(first, res[h]), dots(second, res[h + HALF])
            return tuple(s + a + b for s, a, b in zip(sums, one, two))

        zero = jnp.zeros((rows, 128), f32)
        return lax.fori_loop(0, HALF, plane_chunk, (zero, zero, zero))

    row8 = lax.broadcasted_iota(jnp.int32, (8, 128), 0)
    lane8 = lax.broadcasted_iota(jnp.int32, (8, 128), 1)

    def reduce_all(sweep, sums):
        re, im, norm = [jnp.sum(s, axis=0, keepdims=True) for s in sums]
        red[sweep, 0] = jnp.where(row8 == 0, re, jnp.where(row8 == 1, im, norm))

        def send(d, carry):
            pltpu.make_async_remote_copy(
                src_ref=red.at[sweep, 0], dst_ref=red.at[sweep, d],
                send_sem=s_send.at[sweep], recv_sem=s_recv.at[sweep],
                device_id=device(lax.rem(me + d, total)), device_id_type=MESH).start()
            return carry

        lax.fori_loop(1, total, send, 0)
        everyone = red.at[sweep, pl.ds(1, total - 1)]
        pltpu.make_async_copy(everyone, everyone, s_recv.at[sweep]).wait()
        value = jnp.sum(red[sweep], axis=0)
        for step in (4, 2, 1):
            value = value + jnp.where(lane8 // step % 2 == 0,
                                      pltpu.roll(value, 128 - step, 1), pltpu.roll(value, step, 1))
        real = lane8[:1] < 8 * nrhs
        norm = jnp.where(real, value[2:3], 1.0)
        pltpu.make_async_copy(everyone, everyone, s_send.at[sweep]).wait()
        return value[0:1] / norm, value[1:2] / norm

    def turned(alpha_re, alpha_im, v):
        re, im = v[:, :128], v[:, 128:]
        return jnp.concatenate([alpha_re * re - alpha_im * im, alpha_re * im + alpha_im * re], axis=1)

    for sweep in range(SWEEPS):
        gathers, edges = send_parts(sweep)
        if sweep == 0:
            for m in range(9):
                loads[m].wait()
                place = LOCAL.index(m) if m in LOCAL else ACROSS.index(m)
                target = w_local if m in LOCAL else w_across

                def two_rows(i, carry, m=m, place=place, target=target):
                    flipped = []
                    for a in range(2):
                        both = jnp.concatenate([raw[m, 0, 2 * i + a], raw[m, 1, 2 * i + a]], axis=0)
                        flipped.append(both.astype(f32).T)
                    for g in range(GROUPS):
                        piece = jnp.concatenate([f[8 * g:8 * g + 8] for f in flipped], axis=0)
                        target[g, pl.ds(pl.multiple_of(16 * i, 16), 16),
                               2 * comps * place:2 * comps * (place + 1)] = piece.astype(bf16)
                    return carry

                lax.fori_loop(0, rows // 2, two_rows, 0)
        wait_gather(sweep)
        build_local(sweep)
        apply_local()
        wait_edges(sweep)
        sums = apply_across(sweep)
        alpha_re, alpha_im = reduce_all(sweep, sums)

        def update(g, carry):
            r = res[g]
            step = turned(alpha_re, alpha_im, r)
            sol[g] = step if sweep == 0 else sol[g] + step
            res[g] = r - turned(alpha_re, alpha_im, image[g])
            return carry

        lax.fori_loop(0, GROUPS, update, 0)
        for copy in gathers + edges:
            copy.wait_send()

    for held, out in ((sol, sol_out), (res, res_out)):
        for p in range(2):
            chunks = [held[g, :, 128 * p:128 * p + 128] for g in range(GROUPS)]
            for k in range(nrhs):
                value = chunks[0] if k == 0 else pltpu.roll(chunks[0], -8 * k % 128, 1)
                for g in range(1, GROUPS):
                    shift = 8 * (g - k) % 128
                    moved = chunks[g] if shift == 0 else pltpu.roll(chunks[g], shift, 1)
                    value = jnp.where(lane // 8 == g, moved, value)
                out[p, k] = value


def body(n_grp, n_fold, blocks, source, plane_counts):
    rows, comps = blocks.shape[2], blocks.shape[3]
    nrhs = source.shape[2]
    bf16, f32 = jnp.bfloat16, jnp.float32
    shape = (2, nrhs, rows, GROUPS * CHUNK)
    vmem = pl.BlockSpec(memory_space=pltpu.VMEM)
    total = n_grp * n_fold
    outs = pl.pallas_call(
        functools.partial(kernel, n_grp, n_fold),
        out_shape=(jax.ShapeDtypeStruct(shape, f32), jax.ShapeDtypeStruct(shape, f32)),
        in_specs=[pl.BlockSpec(memory_space=pltpu.SMEM), pl.BlockSpec(memory_space=pl.ANY), vmem, vmem],
        out_specs=(vmem, vmem),
        scratch_shapes=[
            pltpu.VMEM(blocks.shape, bf16),
            pltpu.VMEM((GROUPS, rows * CHUNK, len(LOCAL) * 2 * comps), bf16),
            pltpu.VMEM((GROUPS, rows * CHUNK, len(ACROSS) * 2 * comps), bf16),
            pltpu.VMEM((GROUPS, rows, 256), f32),
            pltpu.VMEM((GROUPS, rows, 256), f32),
            pltpu.VMEM((GROUPS, rows, 256), f32),
            pltpu.VMEM((SWEEPS, n_fold, GROUPS, rows, 256), bf16),
            pltpu.VMEM((SWEEPS, HALF, rows, 256), bf16),
            pltpu.VMEM((SWEEPS, 2, n_fold, HALF, rows, 256), bf16),
            pltpu.VMEM((5, GROUPS, 2 * comps, 256), bf16),
            pltpu.VMEM((SWEEPS, total, 8, 128), f32),
            pltpu.SemaphoreType.DMA((9,)),
            pltpu.SemaphoreType.DMA((SWEEPS, n_fold)),
            pltpu.SemaphoreType.DMA((SWEEPS, n_fold)),
            pltpu.SemaphoreType.DMA((SWEEPS, 2, n_fold)),
            pltpu.SemaphoreType.DMA((SWEEPS, 2, n_fold)),
            pltpu.SemaphoreType.DMA((SWEEPS,)),
            pltpu.SemaphoreType.DMA((SWEEPS,)),
        ],
        compiler_params=pltpu.CompilerParams(
            collective_id=0, has_side_effects=True, vmem_limit_bytes=56 * 1024 * 1024),
    )(plane_counts, blocks, source.transpose(0, 2, 1, 3), lane_moves())
    return tuple(out.transpose(0, 2, 1, 3) for out in outs)


def solution(mesh):
    return jax.shard_map(
        functools.partial(body, mesh.shape["grp"], mesh.shape["fold"]),
        mesh=mesh,
        in_specs=(P(None, None, "fold", None, "grp"), P(None, "fold", None, "grp"), P("grp")),
        out_specs=(P(None, "fold", None, "grp"), P(None, "fold", None, "grp")),
        check_vma=False,
    )
```

```python
import functools

import jax
import jax.numpy as jnp
import numpy as np
from jax import lax
from jax.experimental import pallas as pl
from jax.experimental.pallas import tpu as pltpu
from jax.sharding import PartitionSpec as P

SWEEPS = 2
CHUNK = 8
GROUPS = 16
HALF = GROUPS // 2
LOCAL = (0, 1, 2, 3, 4, 7, 8)
ACROSS = (5, 6)
MESH = pl.DeviceIdType.MESH


def lane_moves():
    moves = np.zeros((256, 512), np.float32)
    for lane in range(128):
        base, site = lane // 8 * 8, lane % 8
        low = site < 4
        moves[base + (site ^ 4) + (0 if low else 128), lane] = 1
        moves[base + (site ^ 4) + (128 if low else 0), 128 + lane] = 1
        moves[base + (site & 4) + ((site + 1) & 3), 256 + lane] = 1
        moves[base + (site & 4) + ((site - 1) & 3), 384 + lane] = 1
    return jnp.asarray(moves, jnp.bfloat16)


def kernel(n_grp, n_fold, counts, blocks, source, moves, sol, res,
           raw, w_local, w_across, image, gath, last, rims, local_rhs, red,
           load_sem, x_send, x_recv, r_send, r_recv, s_send, s_recv):
    bf16, f32 = jnp.bfloat16, jnp.float32
    rows, comps = blocks.shape[2], blocks.shape[3]
    nrhs = source.shape[1]
    total = n_grp * n_fold
    grp, fold = lax.axis_index("grp"), lax.axis_index("fold")
    me = grp * n_fold + fold
    loads = [pltpu.make_async_copy(blocks.at[m], raw.at[m], load_sem.at[m]) for m in range(9)]
    for load in loads:
        load.start()

    def device(index):
        return (lax.div(index, n_fold), lax.rem(index, n_fold))

    barrier = pltpu.get_barrier_semaphore()

    def greet(d, carry):
        pl.semaphore_signal(barrier, inc=1, device_id=device(lax.rem(me + d, total)), device_id_type=MESH)
        return carry

    lax.fori_loop(1, total, greet, 0)

    live = (counts[0] - 1).astype(f32)
    lane = lax.broadcasted_iota(jnp.int32, (rows, 128), 1)

    for p in range(2):
        planes = [source[p, k].astype(f32) for k in range(nrhs)]
        for g in range(GROUPS):
            value = jnp.zeros((rows, 128), f32)
            for k in range(nrhs):
                shift = 8 * (k - g) % 128
                moved = planes[k] if shift == 0 else pltpu.roll(planes[k], shift, 1)
                value = jnp.where(lane // 8 == k, moved, value)
            if g >= HALF:
                value = value * live
            res[g, :, 128 * p:128 * p + 128] = value

    pl.semaphore_wait(barrier, total - 1)

    def send_parts(sweep):
        def fill(h, carry):
            lower, upper = res[h], res[h + HALF]
            gath[sweep, fold, h] = lower.astype(bf16)
            gath[sweep, fold, h + HALF] = upper.astype(bf16)
            last[sweep, h] = (upper * live + lower * (1.0 - live)).astype(bf16)
            return carry

        lax.fori_loop(0, HALF, fill, 0, unroll=2)
        gathers, edges = [], []
        for d in range(1, n_fold):
            gathers.append(pltpu.make_async_remote_copy(
                src_ref=gath.at[sweep, fold], dst_ref=gath.at[sweep, fold],
                send_sem=x_send.at[sweep, d], recv_sem=x_recv.at[sweep, d],
                device_id=(grp, lax.rem(fold + d, n_fold)), device_id_type=MESH))
        for d in range(n_fold):
            other = lax.rem(fold + d, n_fold)
            edges.append(pltpu.make_async_remote_copy(
                src_ref=gath.at[sweep, fold, pl.ds(0, HALF)], dst_ref=rims.at[sweep, 0, fold],
                send_sem=r_send.at[sweep, 0, d], recv_sem=r_recv.at[sweep, 0, d],
                device_id=(lax.rem(grp + n_grp - 1, n_grp), other), device_id_type=MESH))
            edges.append(pltpu.make_async_remote_copy(
                src_ref=last.at[sweep], dst_ref=rims.at[sweep, 1, fold],
                send_sem=r_send.at[sweep, 1, d], recv_sem=r_recv.at[sweep, 1, d],
                device_id=(lax.rem(grp + 1, n_grp), other), device_id_type=MESH))
        for copy in gathers + edges:
            copy.start()
        return gathers, edges

    def wait_gather(sweep):
        for d in range(1, n_fold):
            sender = lax.rem(fold + n_fold - d, n_fold)
            slot = gath.at[sweep, sender]
            pltpu.make_async_remote_copy(
                src_ref=slot, dst_ref=slot, send_sem=x_send.at[sweep, d], recv_sem=x_recv.at[sweep, d],
                device_id=(grp, lax.rem(fold + d, n_fold)), device_id_type=MESH).wait_recv()

    def wait_edges(sweep):
        for side in range(2):
            for d in range(n_fold):
                sender = lax.rem(fold + n_fold - d, n_fold)
                slot = rims.at[sweep, side, sender]
                pltpu.make_async_remote_copy(
                    src_ref=slot, dst_ref=slot, send_sem=r_send.at[sweep, side, d],
                    recv_sem=r_recv.at[sweep, side, d],
                    device_id=(lax.rem(grp + 1, n_grp), fold), device_id_type=MESH).wait_recv()

    def whole_rows(read):
        parts = [read(f) for f in range(n_fold)]
        if rows % 16:
            return jnp.concatenate([part.astype(f32) for part in parts], axis=0).astype(bf16)
        return jnp.concatenate(parts, axis=0)

    def doubled(re, im):
        return jnp.concatenate(
            [jnp.concatenate([re, im], axis=1), jnp.concatenate([-im, re], axis=1)], axis=0)

    def build_local(sweep):
        def pair(h, carry):
            chunks = [whole_rows(lambda f, i=i: gath[sweep, f, 2 * h + i]) for i in range(2)]
            (are, aim), (bre, bim) = [(c[:, :128], c[:, 128:]) for c in chunks]
            local_rhs[0, 2 * h] = doubled(are, aim)
            local_rhs[0, 2 * h + 1] = doubled(bre, bim)
            left = jnp.concatenate([jnp.concatenate([are, aim, bre, bim], axis=0),
                                    jnp.concatenate([bre, bim, are, aim], axis=0)], axis=1)
            moved = jnp.dot(left, moves[...], preferred_element_type=f32).astype(bf16)
            for i in range(2):
                for hop in range(4):
                    cut = moved[2 * comps * i:2 * comps * (i + 1), 128 * hop:128 * hop + 128]
                    local_rhs[1 + hop, 2 * h + i] = doubled(cut[:comps], cut[comps:])
            return carry

        lax.fori_loop(0, HALF, pair, 0, unroll=2)

    row_site = lax.broadcasted_iota(jnp.int32, (rows * CHUNK, 256), 0) % CHUNK
    lane_site = lax.broadcasted_iota(jnp.int32, (rows * CHUNK, 256), 1) % CHUNK

    def same_site(product):
        kept = jnp.where(row_site == lane_site, product, 0.0)
        return jnp.sum(kept.reshape(rows, CHUNK, 256), axis=1)

    def apply_local():
        def chunk(g, carry):
            plane, x, low = g // HALF * HALF, g % HALF // 2, g % 2
            ahead, behind = plane + (x + 1) % 4 * 2 + low, plane + (x + 3) % 4 * 2 + low
            rhs = jnp.concatenate(
                [local_rhs[0, g], local_rhs[0, ahead], local_rhs[0, behind]]
                + [local_rhs[1 + hop, g] for hop in range(4)], axis=0)
            image[g] = same_site(jnp.dot(w_local[g], rhs, preferred_element_type=f32))
            return carry

        lax.fori_loop(0, GROUPS, chunk, 0, unroll=4)

    def dots(a, r):
        are, aim, rre, rim = a[:, :128], a[:, 128:], r[:, :128], r[:, 128:]
        return are * rre + aim * rim, are * rim - aim * rre, are * are + aim * aim

    def apply_across(sweep):
        def plane_chunk(h, sums):
            after = whole_rows(lambda f: rims[sweep, 0, f, h])
            before = whole_rows(lambda f: rims[sweep, 1, f, h])
            after = doubled(after[:, :128], after[:, 128:])
            before = doubled(before[:, :128], before[:, 128:])
            inner, outer = local_rhs[0, h], local_rhs[0, h + HALF]
            up = (outer.astype(f32) * live + after.astype(f32) * (1.0 - live)).astype(bf16)
            first = same_site(jnp.dot(w_across[h], jnp.concatenate([up, before], axis=0),
                                      preferred_element_type=f32))
            second = same_site(jnp.dot(w_across[h + HALF], jnp.concatenate([after, inner], axis=0),
                                       preferred_element_type=f32))
            first = first + image[h]
            second = (second + image[h + HALF]) * live
            image[h] = first
            image[h + HALF] = second
            one, two = dots(first, res[h]), dots(second, res[h + HALF])
            return tuple(s + a + b for s, a, b in zip(sums, one, two))

        zero = jnp.zeros((rows, 128), f32)
        return lax.fori_loop(0, HALF, plane_chunk, (zero, zero, zero), unroll=2)

    row8 = lax.broadcasted_iota(jnp.int32, (8, 128), 0)
    lane8 = lax.broadcasted_iota(jnp.int32, (8, 128), 1)

    def reduce_all(sweep, sums):
        re, im, norm = [jnp.sum(s, axis=0, keepdims=True) for s in sums]
        red[sweep, 0] = jnp.where(row8 == 0, re, jnp.where(row8 == 1, im, norm))

        def send(d, carry):
            pltpu.make_async_remote_copy(
                src_ref=red.at[sweep, 0], dst_ref=red.at[sweep, d],
                send_sem=s_send.at[sweep], recv_sem=s_recv.at[sweep],
                device_id=device(lax.rem(me + d, total)), device_id_type=MESH).start()
            return carry

        lax.fori_loop(1, total, send, 0)
        everyone = red.at[sweep, pl.ds(1, total - 1)]
        pltpu.make_async_copy(everyone, everyone, s_recv.at[sweep]).wait()
        value = jnp.sum(red[sweep], axis=0)
        for step in (4, 2, 1):
            value = value + jnp.where(lane8 // step % 2 == 0,
                                      pltpu.roll(value, 128 - step, 1), pltpu.roll(value, step, 1))
        real = lane8[:1] < 8 * nrhs
        norm = jnp.where(real, value[2:3], 1.0)
        pltpu.make_async_copy(everyone, everyone, s_send.at[sweep]).wait()
        return value[0:1] / norm, value[1:2] / norm

    def turned(alpha_re, alpha_im, v):
        re, im = v[:, :128], v[:, 128:]
        return jnp.concatenate([alpha_re * re - alpha_im * im, alpha_re * im + alpha_im * re], axis=1)

    for sweep in range(SWEEPS):
        gathers, edges = send_parts(sweep)
        if sweep == 0:
            for m in range(9):
                loads[m].wait()
                place = LOCAL.index(m) if m in LOCAL else ACROSS.index(m)
                target = w_local if m in LOCAL else w_across

                def two_rows(i, carry, m=m, place=place, target=target):
                    flipped = []
                    for a in range(2):
                        both = jnp.concatenate([raw[m, 0, 2 * i + a], raw[m, 1, 2 * i + a]], axis=0)
                        flipped.append(both.T.astype(f32))
                    for g in range(GROUPS):
                        piece = jnp.concatenate([f[8 * g:8 * g + 8] for f in flipped], axis=0)
                        target[g, pl.ds(pl.multiple_of(16 * i, 16), 16),
                               2 * comps * place:2 * comps * (place + 1)] = piece.astype(bf16)
                    return carry

                lax.fori_loop(0, rows // 2, two_rows, 0, unroll=4)
        wait_gather(sweep)
        build_local(sweep)
        apply_local()
        wait_edges(sweep)
        sums = apply_across(sweep)
        alpha_re, alpha_im = reduce_all(sweep, sums)

        def update(g, carry):
            r = res[g]
            step = turned(alpha_re, alpha_im, r)
            sol[g] = step if sweep == 0 else sol[g] + step
            res[g] = r - turned(alpha_re, alpha_im, image[g])
            return carry

        lax.fori_loop(0, GROUPS, update, 0, unroll=4)
        for copy in gathers + edges:
            copy.wait_send()


def finish(sol, res, sol_out, res_out):
    nrhs = sol_out.shape[1]
    lane = lax.broadcasted_iota(jnp.int32, (sol.shape[1], 128), 1)
    for held, out in ((sol, sol_out), (res, res_out)):
        for p in range(2):
            chunks = [held[g, :, 128 * p:128 * p + 128] for g in range(GROUPS)]
            for k in range(nrhs):
                value = chunks[0] if k == 0 else pltpu.roll(chunks[0], -8 * k % 128, 1)
                for g in range(1, GROUPS):
                    shift = 8 * (g - k) % 128
                    moved = chunks[g] if shift == 0 else pltpu.roll(chunks[g], shift, 1)
                    value = jnp.where(lane // 8 == g, moved, value)
                out[p, k] = value


def body(n_grp, n_fold, blocks, source, plane_counts):
    rows, comps = blocks.shape[2], blocks.shape[3]
    nrhs = source.shape[2]
    bf16, f32 = jnp.bfloat16, jnp.float32
    shape = (2, nrhs, rows, GROUPS * CHUNK)
    vmem = pl.BlockSpec(memory_space=pltpu.VMEM)
    total = n_grp * n_fold
    held = jax.ShapeDtypeStruct((GROUPS, rows, 256), f32)
    iterate = pl.pallas_call(
        functools.partial(kernel, n_grp, n_fold),
        out_shape=(held, held),
        in_specs=[pl.BlockSpec(memory_space=pltpu.SMEM), pl.BlockSpec(memory_space=pl.ANY), vmem, vmem],
        out_specs=(vmem, vmem),
        scratch_shapes=[
            pltpu.VMEM(blocks.shape, bf16),
            pltpu.VMEM((GROUPS, rows * CHUNK, len(LOCAL) * 2 * comps), bf16),
            pltpu.VMEM((GROUPS, rows * CHUNK, len(ACROSS) * 2 * comps), bf16),
            pltpu.VMEM((GROUPS, rows, 256), f32),
            pltpu.VMEM((SWEEPS, n_fold, GROUPS, rows, 256), bf16),
            pltpu.VMEM((SWEEPS, HALF, rows, 256), bf16),
            pltpu.VMEM((SWEEPS, 2, n_fold, HALF, rows, 256), bf16),
            pltpu.VMEM((5, GROUPS, 2 * comps, 256), bf16),
            pltpu.VMEM((SWEEPS, total, 8, 128), f32),
            pltpu.SemaphoreType.DMA((9,)),
            pltpu.SemaphoreType.DMA((SWEEPS, n_fold)),
            pltpu.SemaphoreType.DMA((SWEEPS, n_fold)),
            pltpu.SemaphoreType.DMA((SWEEPS, 2, n_fold)),
            pltpu.SemaphoreType.DMA((SWEEPS, 2, n_fold)),
            pltpu.SemaphoreType.DMA((SWEEPS,)),
            pltpu.SemaphoreType.DMA((SWEEPS,)),
        ],
        compiler_params=pltpu.CompilerParams(
            collective_id=0, has_side_effects=True, vmem_limit_bytes=56 * 1024 * 1024),
    )(plane_counts, blocks, source.transpose(0, 2, 1, 3), lane_moves())
    outs = pl.pallas_call(
        finish,
        out_shape=(jax.ShapeDtypeStruct(shape, f32), jax.ShapeDtypeStruct(shape, f32)),
        in_specs=[vmem, vmem],
        out_specs=(vmem, vmem),
    )(*iterate)
    return tuple(out.transpose(0, 2, 1, 3) for out in outs)


def solution(mesh):
    return jax.shard_map(
        functools.partial(body, mesh.shape["grp"], mesh.shape["fold"]),
        mesh=mesh,
        in_specs=(P(None, None, "fold", None, "grp"), P(None, "fold", None, "grp"), P("grp")),
        out_specs=(P(None, "fold", None, "grp"), P(None, "fold", None, "grp")),
        check_vma=False,
    )
```

```python
import functools

import jax
import jax.numpy as jnp
import numpy as np
from jax import lax
from jax.experimental import pallas as pl
from jax.experimental.pallas import tpu as pltpu
from jax.sharding import PartitionSpec as P

SWEEPS = 2
CHUNK = 8
GROUPS = 16
HALF = GROUPS // 2
LOCAL = (0, 1, 2, 3, 4, 7, 8)
ACROSS = (5, 6)
MESH = pl.DeviceIdType.MESH


def lane_moves():
    moves = np.zeros((256, 512), np.float32)
    for lane in range(128):
        base, site = lane // 8 * 8, lane % 8
        low = site < 4
        moves[base + (site ^ 4) + (0 if low else 128), lane] = 1
        moves[base + (site ^ 4) + (128 if low else 0), 128 + lane] = 1
        moves[base + (site & 4) + ((site + 1) & 3), 256 + lane] = 1
        moves[base + (site & 4) + ((site - 1) & 3), 384 + lane] = 1
    return jnp.asarray(moves, jnp.bfloat16)


def kernel(n_grp, n_fold, counts, blocks, source, moves, sol, res,
           raw, w_local, w_across, image, gath, last, rims, local_rhs, red,
           load_sem, x_send, x_recv, r_send, r_recv, s_send, s_recv):
    bf16, f32 = jnp.bfloat16, jnp.float32
    rows, comps = blocks.shape[2], blocks.shape[3]
    nrhs = source.shape[1]
    total = n_grp * n_fold
    grp, fold = lax.axis_index("grp"), lax.axis_index("fold")
    me = grp * n_fold + fold
    loads = [pltpu.make_async_copy(blocks.at[m], raw.at[m], load_sem.at[m]) for m in range(9)]
    for load in loads:
        load.start()

    def device(index):
        return (lax.div(index, n_fold), lax.rem(index, n_fold))

    barrier = pltpu.get_barrier_semaphore()

    def greet(d, carry):
        pl.semaphore_signal(barrier, inc=1, device_id=device(lax.rem(me + d, total)), device_id_type=MESH)
        return carry

    lax.fori_loop(1, total, greet, 0)

    live = (counts[0] - 1).astype(f32)
    lane = lax.broadcasted_iota(jnp.int32, (rows, 128), 1)

    for p in range(2):
        planes = [source[p, k].astype(f32) for k in range(nrhs)]
        for g in range(GROUPS):
            value = jnp.zeros((rows, 128), f32)
            for k in range(nrhs):
                shift = 8 * (k - g) % 128
                moved = planes[k] if shift == 0 else pltpu.roll(planes[k], shift, 1)
                value = jnp.where(lane // 8 == k, moved, value)
            if g >= HALF:
                value = value * live
            res[g, :, 128 * p:128 * p + 128] = value

    pl.semaphore_wait(barrier, total - 1)

    def send_parts(sweep):
        def fill(h, carry):
            lower, upper = res[h], res[h + HALF]
            gath[sweep, fold, h] = lower.astype(bf16)
            gath[sweep, fold, h + HALF] = upper.astype(bf16)
            last[sweep, h] = (upper * live + lower * (1.0 - live)).astype(bf16)
            return carry

        lax.fori_loop(0, HALF, fill, 0, unroll=2)
        gathers, edges = [], []
        for d in range(1, n_fold):
            gathers.append(pltpu.make_async_remote_copy(
                src_ref=gath.at[sweep, fold], dst_ref=gath.at[sweep, fold],
                send_sem=x_send.at[sweep, d], recv_sem=x_recv.at[sweep, d],
                device_id=(grp, lax.rem(fold + d, n_fold)), device_id_type=MESH))
        for side, src, step in ((0, gath.at[sweep, fold, pl.ds(0, HALF)], n_grp - 1), (1, last.at[sweep], 1)):
            edges.append(pltpu.make_async_remote_copy(
                src_ref=src, dst_ref=rims.at[sweep, side, fold],
                send_sem=r_send.at[sweep, side, 0], recv_sem=r_recv.at[sweep, side, 0],
                device_id=(lax.rem(grp + step, n_grp), fold), device_id_type=MESH))
        for copy in edges + gathers:
            copy.start()
        return gathers, edges

    def wait_gather(sweep):
        for d in range(1, n_fold):
            sender = lax.rem(fold + n_fold - d, n_fold)
            slot = gath.at[sweep, sender]
            pltpu.make_async_remote_copy(
                src_ref=slot, dst_ref=slot, send_sem=x_send.at[sweep, d], recv_sem=x_recv.at[sweep, d],
                device_id=(grp, lax.rem(fold + d, n_fold)), device_id_type=MESH).wait_recv()

    def forward(sweep, side, d, sender):
        slot = rims.at[sweep, side, sender]
        return pltpu.make_async_remote_copy(
            src_ref=slot, dst_ref=slot, send_sem=r_send.at[sweep, side, d],
            recv_sem=r_recv.at[sweep, side, d],
            device_id=(grp, lax.rem(fold + d, n_fold)), device_id_type=MESH)

    def pass_edges(sweep, edges):
        passed = []
        for side in range(2):
            edges[side].wait_recv()
            passed += [forward(sweep, side, d, fold) for d in range(1, n_fold)]
            for copy in passed[-(n_fold - 1):]:
                copy.start()
        return passed

    def wait_edges(sweep):
        for side in range(2):
            for d in range(1, n_fold):
                forward(sweep, side, d, lax.rem(fold + n_fold - d, n_fold)).wait_recv()

    def whole_rows(read):
        parts = [read(f) for f in range(n_fold)]
        if rows % 16:
            return jnp.concatenate([part.astype(f32) for part in parts], axis=0).astype(bf16)
        return jnp.concatenate(parts, axis=0)

    def doubled(re, im):
        return jnp.concatenate(
            [jnp.concatenate([re, im], axis=1), jnp.concatenate([-im, re], axis=1)], axis=0)

    def build_local(sweep):
        def pair(h, carry):
            chunks = [whole_rows(lambda f, i=i: gath[sweep, f, 2 * h + i]) for i in range(2)]
            (are, aim), (bre, bim) = [(c[:, :128], c[:, 128:]) for c in chunks]
            local_rhs[0, 2 * h] = doubled(are, aim)
            local_rhs[0, 2 * h + 1] = doubled(bre, bim)
            left = jnp.concatenate([jnp.concatenate([are, aim, bre, bim], axis=0),
                                    jnp.concatenate([bre, bim, are, aim], axis=0)], axis=1)
            moved = jnp.dot(left, moves[...], preferred_element_type=f32).astype(bf16)
            for i in range(2):
                for hop in range(4):
                    cut = moved[2 * comps * i:2 * comps * (i + 1), 128 * hop:128 * hop + 128]
                    local_rhs[1 + hop, 2 * h + i] = doubled(cut[:comps], cut[comps:])
            return carry

        lax.fori_loop(0, HALF, pair, 0, unroll=2)

    row_site = lax.broadcasted_iota(jnp.int32, (rows * CHUNK, 256), 0) % CHUNK
    lane_site = lax.broadcasted_iota(jnp.int32, (rows * CHUNK, 256), 1) % CHUNK

    def same_site(product):
        kept = jnp.where(row_site == lane_site, product, 0.0)
        return jnp.sum(kept.reshape(rows, CHUNK, 256), axis=1)

    def apply_local(begin, end):
        def chunk(g, carry):
            plane, x, low = g // HALF * HALF, g % HALF // 2, g % 2
            ahead, behind = plane + (x + 1) % 4 * 2 + low, plane + (x + 3) % 4 * 2 + low
            rhs = jnp.concatenate(
                [local_rhs[0, g], local_rhs[0, ahead], local_rhs[0, behind]]
                + [local_rhs[1 + hop, g] for hop in range(4)], axis=0)
            image[g] = same_site(jnp.dot(w_local[g], rhs, preferred_element_type=f32))
            return carry

        lax.fori_loop(begin, end, chunk, 0, unroll=8)

    def dots(a, r):
        are, aim, rre, rim = a[:, :128], a[:, 128:], r[:, :128], r[:, 128:]
        return are * rre + aim * rim, are * rim - aim * rre, are * are + aim * aim

    def apply_across(sweep):
        def plane_chunk(h, sums):
            after = whole_rows(lambda f: rims[sweep, 0, f, h])
            before = whole_rows(lambda f: rims[sweep, 1, f, h])
            after = doubled(after[:, :128], after[:, 128:])
            before = doubled(before[:, :128], before[:, 128:])
            inner, outer = local_rhs[0, h], local_rhs[0, h + HALF]
            up = (outer.astype(f32) * live + after.astype(f32) * (1.0 - live)).astype(bf16)
            first = same_site(jnp.dot(w_across[h], jnp.concatenate([up, before], axis=0),
                                      preferred_element_type=f32))
            second = same_site(jnp.dot(w_across[h + HALF], jnp.concatenate([after, inner], axis=0),
                                       preferred_element_type=f32))
            first = first + image[h]
            second = (second + image[h + HALF]) * live
            image[h] = first
            image[h + HALF] = second
            one, two = dots(first, res[h]), dots(second, res[h + HALF])
            return tuple(s + a + b for s, a, b in zip(sums, one, two))

        zero = jnp.zeros((rows, 128), f32)
        return lax.fori_loop(0, HALF, plane_chunk, (zero, zero, zero), unroll=4)

    row8 = lax.broadcasted_iota(jnp.int32, (8, 128), 0)
    lane8 = lax.broadcasted_iota(jnp.int32, (8, 128), 1)

    def reduce_all(sweep, sums):
        re, im, norm = [jnp.sum(s, axis=0, keepdims=True) for s in sums]
        red[sweep, 0] = jnp.where(row8 == 0, re, jnp.where(row8 == 1, im, norm))

        def send(d, carry):
            pltpu.make_async_remote_copy(
                src_ref=red.at[sweep, 0], dst_ref=red.at[sweep, d],
                send_sem=s_send.at[sweep], recv_sem=s_recv.at[sweep],
                device_id=device(lax.rem(me + d, total)), device_id_type=MESH).start()
            return carry

        lax.fori_loop(1, total, send, 0)
        everyone = red.at[sweep, pl.ds(1, total - 1)]
        pltpu.make_async_copy(everyone, everyone, s_recv.at[sweep]).wait()
        value = jnp.sum(red[sweep], axis=0)
        for step in (4, 2, 1):
            value = value + jnp.where(lane8 // step % 2 == 0,
                                      pltpu.roll(value, 128 - step, 1), pltpu.roll(value, step, 1))
        real = lane8[:1] < 8 * nrhs
        norm = jnp.where(real, value[2:3], 1.0)
        pltpu.make_async_copy(everyone, everyone, s_send.at[sweep]).wait()
        return value[0:1] / norm, value[1:2] / norm

    def turned(alpha_re, alpha_im, v):
        re, im = v[:, :128], v[:, 128:]
        return jnp.concatenate([alpha_re * re - alpha_im * im, alpha_re * im + alpha_im * re], axis=1)

    for sweep in range(SWEEPS):
        gathers, edges = send_parts(sweep)
        if sweep == 0:
            for m in range(9):
                loads[m].wait()
                place = LOCAL.index(m) if m in LOCAL else ACROSS.index(m)
                target = w_local if m in LOCAL else w_across

                def two_rows(i, carry, m=m, place=place, target=target):
                    flipped = []
                    for a in range(2):
                        both = jnp.concatenate([raw[m, 0, 2 * i + a], raw[m, 1, 2 * i + a]], axis=0)
                        flipped.append(both.T.astype(f32))
                    for g in range(GROUPS):
                        piece = jnp.concatenate([f[8 * g:8 * g + 8] for f in flipped], axis=0)
                        target[g, pl.ds(pl.multiple_of(16 * i, 16), 16),
                               2 * comps * place:2 * comps * (place + 1)] = piece.astype(bf16)
                    return carry

                lax.fori_loop(0, rows // 2, two_rows, 0, unroll=4)
            passed = pass_edges(sweep, edges)
        wait_gather(sweep)
        build_local(sweep)
        apply_local(0, HALF)
        if sweep > 0:
            passed = pass_edges(sweep, edges)
        apply_local(HALF, GROUPS)
        wait_edges(sweep)
        sums = apply_across(sweep)
        alpha_re, alpha_im = reduce_all(sweep, sums)

        def update(g, carry):
            r = res[g]
            step = turned(alpha_re, alpha_im, r)
            sol[g] = step if sweep == 0 else sol[g] + step
            res[g] = r - turned(alpha_re, alpha_im, image[g])
            return carry

        lax.fori_loop(0, GROUPS, update, 0, unroll=4)
        for copy in gathers + edges + passed:
            copy.wait_send()


def finish(sol, res, sol_out, res_out):
    nrhs = sol_out.shape[1]
    lane = lax.broadcasted_iota(jnp.int32, (sol.shape[1], 128), 1)
    for held, out in ((sol, sol_out), (res, res_out)):
        for p in range(2):
            chunks = [held[g, :, 128 * p:128 * p + 128] for g in range(GROUPS)]
            for k in range(nrhs):
                value = chunks[0] if k == 0 else pltpu.roll(chunks[0], -8 * k % 128, 1)
                for g in range(1, GROUPS):
                    shift = 8 * (g - k) % 128
                    moved = chunks[g] if shift == 0 else pltpu.roll(chunks[g], shift, 1)
                    value = jnp.where(lane // 8 == g, moved, value)
                out[p, k] = value


def body(n_grp, n_fold, blocks, source, plane_counts):
    rows, comps = blocks.shape[2], blocks.shape[3]
    nrhs = source.shape[2]
    bf16, f32 = jnp.bfloat16, jnp.float32
    shape = (2, nrhs, rows, GROUPS * CHUNK)
    vmem = pl.BlockSpec(memory_space=pltpu.VMEM)
    total = n_grp * n_fold
    held = jax.ShapeDtypeStruct((GROUPS, rows, 256), f32)
    iterate = pl.pallas_call(
        functools.partial(kernel, n_grp, n_fold),
        out_shape=(held, held),
        in_specs=[pl.BlockSpec(memory_space=pltpu.SMEM), pl.BlockSpec(memory_space=pl.ANY), vmem, vmem],
        out_specs=(vmem, vmem),
        scratch_shapes=[
            pltpu.VMEM(blocks.shape, bf16),
            pltpu.VMEM((GROUPS, rows * CHUNK, len(LOCAL) * 2 * comps), bf16),
            pltpu.VMEM((GROUPS, rows * CHUNK, len(ACROSS) * 2 * comps), bf16),
            pltpu.VMEM((GROUPS, rows, 256), f32),
            pltpu.VMEM((SWEEPS, n_fold, GROUPS, rows, 256), bf16),
            pltpu.VMEM((SWEEPS, HALF, rows, 256), bf16),
            pltpu.VMEM((SWEEPS, 2, n_fold, HALF, rows, 256), bf16),
            pltpu.VMEM((5, GROUPS, 2 * comps, 256), bf16),
            pltpu.VMEM((SWEEPS, total, 8, 128), f32),
            pltpu.SemaphoreType.DMA((9,)),
            pltpu.SemaphoreType.DMA((SWEEPS, n_fold)),
            pltpu.SemaphoreType.DMA((SWEEPS, n_fold)),
            pltpu.SemaphoreType.DMA((SWEEPS, 2, n_fold)),
            pltpu.SemaphoreType.DMA((SWEEPS, 2, n_fold)),
            pltpu.SemaphoreType.DMA((SWEEPS,)),
            pltpu.SemaphoreType.DMA((SWEEPS,)),
        ],
        compiler_params=pltpu.CompilerParams(
            collective_id=0, has_side_effects=True, vmem_limit_bytes=56 * 1024 * 1024),
    )(plane_counts, blocks, source.transpose(0, 2, 1, 3), lane_moves())
    outs = pl.pallas_call(
        finish,
        out_shape=(jax.ShapeDtypeStruct(shape, f32), jax.ShapeDtypeStruct(shape, f32)),
        in_specs=[vmem, vmem],
        out_specs=(vmem, vmem),
    )(*iterate)
    return tuple(out.transpose(0, 2, 1, 3) for out in outs)


def solution(mesh):
    return jax.shard_map(
        functools.partial(body, mesh.shape["grp"], mesh.shape["fold"]),
        mesh=mesh,
        in_specs=(P(None, None, "fold", None, "grp"), P(None, "fold", None, "grp"), P("grp")),
        out_specs=(P(None, "fold", None, "grp"), P(None, "fold", None, "grp")),
        check_vma=False,
    )
```
